32 devices in a mesh: row: 4 (over y, core), col: 8 (over z, x).
Axes of the slice: x: 2, y: 2, z: 4, core: 2. Of those that a mesh axis runs over, the one named last changes fastest.
Arguments:
- tokens: bfloat16 [2048, 8192], P('col', 'row'), may hold values from -6 to 6
- grad_out: bfloat16 [2048, 16384], P('row', 'col'), may hold values from -6 to 6
- base_weight: float32 [8192, 16384], P('row', 'col'), may hold values from -6 to 6
- left_param: float32 [16, 512, 512], P('row'), may hold values from -6 to 6
- right_param: float32 [64, 256, 256], P('col'), may hold values from -6 to 6
Outputs:
- rotated_weight: float32 [8192, 16384], P('row', 'col')
- new_left: float32 [16, 512, 512], P('row')
- new_right: float32 [64, 256, 256], P('col')
The draws below stay inside these ranges and needn't reach their ends.
All inputs are finite; a program needn't handle non-finite values.
Results may differ from the reference program's by a relative error of at most 0.0003.
Values may be sent and summed in bfloat16 or wider, within the bound.
No kernel may reach another device: no remote copies, remote signals or barrier semaphores. Data moves between devices by JAX's collectives and lax.ppermute only.
A program may use at most 192 MiB of HBM per device.

```python
import math
import jax
import jax.numpy as jnp
from jax import lax

D = 8192
FF = 16384
LBLK = 512
RBLK = 256
TOKENS = 2048


def level_of(key, extent, split, least, largest):
    def one(position, blocks):
        draws = jax.random.uniform(jax.random.fold_in(jax.random.fold_in(key, 6), position), (blocks,), jnp.float32, least / len(split), largest / len(split))
        return jnp.repeat(jnp.exp(draws), extent[position] // blocks).reshape((-1,) + (1,) * (len(extent) - position - 1))

    gain = one(*split[0])
    for cut in split[1:]:
        gain = gain * one(*cut)
    return gain


def centred(rng, dims, scale, most, pieces=(), kind=jnp.bfloat16):
    result = jax.random.normal(rng, dims, jnp.float32) * scale
    if len(pieces) > 0:
        result = level_of(rng, dims, pieces, -0.22, 0.18) * result
    return jnp.clip(result, min=-most, max=most).astype(kind)


def setup_inputs(seed: int = 0) -> dict:
    key_list = jax.random.split(jax.random.key(seed), 6)
    tokens = centred(key_list[0], (TOKENS, D), 1.0, 6.0, ((0, 8), (1, 4)))
    grad_out = centred(key_list[1], (TOKENS, FF), 1.0, 6.0, ((0, 4), (1, 8)))
    base_weight = centred(key_list[2], (D, FF), 1.0, 6.0, ((0, 4), (1, 8)), jnp.float32)
    left_param = centred(key_list[3], (D // LBLK, LBLK, LBLK), 1.0, 6.0, ((0, 4),), jnp.float32)
    right_param = centred(key_list[4], (FF // RBLK, RBLK, RBLK), 1.0, 6.0, ((0, 8),), jnp.float32)
    return {"tokens": tokens, "grad_out": grad_out, "base_weight": base_weight, "left_param": left_param, "right_param": right_param}


precise = lax.Precision.HIGHEST
taylor_degree = 6
step_rate = 0.3
epsilon = 1e-06

def batch_product(first, second):
    return jnp.einsum('lab,lbc->lac', first, second, precision=precise)

def transpose_last(matrix):
    return jnp.swapaxes(matrix, 1, 2)

def skew_from(param):
    skew_scale = 0.5 / math.sqrt(param.shape[-1])
    return skew_scale * (param - transpose_last(param))

def column_levels(skew, col_start, col_width):
    dimension = skew.shape[-1]
    eye_part = (jnp.arange(dimension)[:, None] == col_start + jnp.arange(col_width)[None, :]).astype(jnp.float32)
    current = eye_part[None] + lax.dynamic_slice_in_dim(skew, col_start, col_width, 2) / taylor_degree
    horner_levels = [current] * (taylor_degree + 1)
    for divisor in range(taylor_degree - 1, 0, -1):
        current = eye_part[None] + batch_product(skew, current) / divisor
        horner_levels[divisor] = current
    return horner_levels

def adjoint(skew, horner_levels, upper_grad):
    running = jnp.zeros(skew.shape, jnp.float32)
    for divisor in range(1, taylor_degree):
        running = running + batch_product(upper_grad, transpose_last(horner_levels[divisor + 1])) / divisor
        upper_grad = batch_product(transpose_last(skew), upper_grad) / divisor
    return (running, upper_grad)

def update_param(param, accum):
    skew_scale = 0.5 / math.sqrt(param.shape[-1])
    grad_param = skew_scale * (accum - transpose_last(accum))
    root_mean = jnp.sqrt(lax.optimization_barrier(jnp.mean(grad_param * grad_param, axis=(1, 2), keepdims=True)) + epsilon)
    return param - step_rate * grad_param / root_mean

def right_apply(weight, rotation):
    count = rotation.shape[0]
    block = rotation.shape[-1]
    shaped = weight.reshape(weight.shape[0], count, block)
    return jnp.einsum('nbr,brs->nbs', shaped, rotation, precision=precise).reshape(weight.shape)

def reference(tokens, grad_out, base_weight, left_param, right_param):
    left_skew = skew_from(left_param)
    right_skew = skew_from(right_param)
    left_levels = column_levels(left_skew, 0, LBLK)
    right_levels = column_levels(right_skew, 0, RBLK)
    left_rot = left_levels[1]
    right_rot = right_levels[1]
    left_count = D // LBLK
    right_count = FF // RBLK

    def per_block(carried, block_index):
        weight = lax.dynamic_slice_in_dim(base_weight, block_index * LBLK, LBLK, 0)
        token_rows = lax.dynamic_slice_in_dim(tokens, block_index * LBLK, LBLK, 1)
        rotation = lax.dynamic_index_in_dim(left_rot, block_index, 0, keepdims=False)
        grad_weight = jnp.dot(token_rows.T, grad_out, preferred_element_type=jnp.float32)
        mixed_weight = right_apply(weight, right_rot)
        left_part = jnp.dot(grad_weight, mixed_weight.T, precision=precise)
        rotated = jnp.dot(rotation, weight, precision=precise)
        right_part = jnp.einsum('nbr,nbs->brs', rotated.reshape(LBLK, right_count, RBLK), grad_weight.reshape(LBLK, right_count, RBLK), precision=precise)
        return (carried + right_part, left_part)
    start_right = jnp.zeros((right_count, RBLK, RBLK), jnp.float32)
    right_grad, left_grad = lax.scan(per_block, start_right, jnp.arange(left_count, dtype=jnp.int32))
    left_acc, left_upper = adjoint(left_skew, left_levels, left_grad)
    left_acc = left_acc + left_upper / taylor_degree
    right_acc, right_upper = adjoint(right_skew, right_levels, right_grad)
    right_acc = right_acc + right_upper / taylor_degree
    new_left = update_param(left_param, left_acc)
    new_right = update_param(right_param, right_acc)
    new_left_rot = column_levels(skew_from(new_left), 0, LBLK)[1]
    new_right_rot = column_levels(skew_from(new_right), 0, RBLK)[1]

    def rotate_block(carried, block_index):
        weight = lax.dynamic_slice_in_dim(base_weight, block_index * LBLK, LBLK, 0)
        rotation = lax.dynamic_index_in_dim(new_left_rot, block_index, 0, keepdims=False)
        turned = jnp.dot(rotation, weight, precision=precise)
        return (carried, right_apply(turned, new_right_rot))
    unused, turned_blocks = lax.scan(rotate_block, jnp.zeros((), jnp.float32), jnp.arange(left_count, dtype=jnp.int32))
    rotated_weight = turned_blocks.reshape(D, FF)
    return (rotated_weight, new_left, new_right)
```

```python
import functools
import math

import jax
import jax.numpy as jnp
from jax import lax
from jax.experimental import pallas as pl
from jax.experimental.pallas import tpu as pltpu
from jax.sharding import PartitionSpec as P

step_rate = 0.3
epsilon = 1e-06
f32 = jnp.float32
bf16 = jnp.bfloat16
VMEM_BYTES = 52 * 1024 * 1024


def params(count=1):
    return pltpu.CompilerParams(
        dimension_semantics=("arbitrary",) * count, vmem_limit_bytes=VMEM_BYTES
    )


def cost(macs, moved):
    return pl.CostEstimate(flops=int(2 * macs), bytes_accessed=int(moved), transcendentals=0)


def split(value):
    high = value.astype(bf16)
    return high, (value - high.astype(f32)).astype(bf16)


def mul(first, second, dims=((1,), (0,))):
    def one(a, b):
        return lax.dot_general(a, b, (dims, ((), ())), preferred_element_type=f32)

    return one(first[0], second[0]) + (one(first[0], second[1]) + one(first[1], second[0]))


def eye(order):
    row = lax.broadcasted_iota(jnp.int32, (order, order), 0)
    col = lax.broadcasted_iota(jnp.int32, (order, order), 1)
    return jnp.where(row == col, 1.0, 0.0).astype(f32)


def skew_of(param):
    return (0.5 / math.sqrt(param.shape[-1])) * (param - param.T)


def exponentials(skews):
    halves = [split(s) for s in skews]
    second = [mul(h, h) for h in halves]
    third = [mul(h, split(p)) for h, p in zip(halves, second)]
    unit = eye(skews[0].shape[-1])
    tails = [
        split(unit / 6 + s / 24 + p / 120 + c / 720) for s, p, c in zip(skews, second, third)
    ]
    return [
        unit + s + p / 2 + mul(split(c), t)
        for s, p, c, t in zip(skews, second, third, tails)
    ]


def pack(skew):
    half = skew.shape[-1] // 2
    row = lax.broadcasted_iota(jnp.int32, (half, half), 0)
    col = lax.broadcasted_iota(jnp.int32, (half, half), 1)
    mixed = jnp.where(row < col, skew[:half, :half], skew[half:, half:])
    return mixed, skew[:half, half:]


def unpack(packed):
    half = packed.shape[0]
    row = lax.broadcasted_iota(jnp.int32, (half, half), 0)
    col = lax.broadcasted_iota(jnp.int32, (half, half), 1)
    mixed = packed[:, :half]
    upper = packed[:, half:]
    first = jnp.where(row < col, mixed, 0.0)
    last = jnp.where(row > col, mixed, 0.0)
    return jnp.concatenate(
        [
            jnp.concatenate([first - first.T, upper], 1),
            jnp.concatenate([-upper.T, last - last.T], 1),
        ],
        0,
    )


def right_kernel(many, updates, *refs):
    if updates:
        order, param, packed, new, high, low = refs
        base = pl.program_id(0) * many
        values = []
        for b in range(many):
            value = param[b] - step_rate * unpack(packed[order[base + b]])
            new[b] = value
            values.append(value)
    else:
        param, high, low = refs
        values = [param[b] for b in range(many)]
    for b, value in enumerate(exponentials([skew_of(v) for v in values])):
        high[b], low[b] = split(value)


def right_rotations(param, packed=None, order=None):
    count, n, _ = param.shape
    many = math.gcd(count, 4)
    updates = packed is not None
    block = pl.BlockSpec((many, n, n), lambda i, *_: (i, 0, 0))
    half = jax.ShapeDtypeStruct((count, n, n), bf16)
    in_specs, outs = [block], [half, half]
    if updates:
        in_specs.append(pl.BlockSpec(packed.shape, lambda i, *_: (0, 0, 0)))
        outs.insert(0, jax.ShapeDtypeStruct((count, n, n), f32))
    call = pl.pallas_call(
        functools.partial(right_kernel, many, updates),
        grid_spec=pltpu.PrefetchScalarGridSpec(
            num_scalar_prefetch=1 if updates else 0,
            grid=(count // many,),
            in_specs=in_specs,
            out_specs=[block] * len(outs),
        ),
        out_shape=outs,
        compiler_params=params(),
        cost_estimate=cost(count * 9 * n**3, count * n * n * 12),
        name="right_rotations",
    )
    return call(order, param, packed) if updates else call(param)


def prep_kernel(param, weight, rot_h, rot_l, m_h, m_l, v_h, v_l, skew, left_h, left_l):
    @pl.when(pl.program_id(0) == 0)
    def _():
        value = skew_of(param[0])
        skew[...] = value
        (rotation,) = exponentials([value])
        left_h[...], left_l[...] = split(rotation)

    halves = split(weight[...])
    n = rot_h.shape[-1]
    for b in range(rot_h.shape[0]):
        cut = slice(b * n, (b + 1) * n)
        value = mul((halves[0][:, cut], halves[1][:, cut]), (rot_h[b], rot_l[b]))
        m_h[:, cut], m_l[:, cut] = split(value)
    high, low = split(mul((left_h[...], left_l[...]), halves))
    v_h[...] = high.T
    v_l[...] = low.T


def prepare(i, left_param, weight, rotations, tile):
    size = left_param.shape[-1]
    cols = weight.shape[1]
    n = rotations[0].shape[-1]
    rot_spec = pl.BlockSpec((tile // n, n, n), lambda j: (j, 0, 0))
    wide = pl.BlockSpec((size, tile), lambda j: (0, j))
    tall = pl.BlockSpec((tile, size), lambda j: (j, 0))
    return pl.pallas_call(
        prep_kernel,
        grid=(cols // tile,),
        in_specs=[
            pl.BlockSpec((1, size, size), lambda j: (i, 0, 0)),
            pl.BlockSpec((size, tile), lambda j: (i, j)),
            rot_spec,
            rot_spec,
        ],
        out_specs=[
            wide,
            wide,
            tall,
            tall,
            pl.BlockSpec((size, size), lambda j: (0, 0)),
        ],
        out_shape=[jax.ShapeDtypeStruct((size, cols), bf16)] * 2
        + [jax.ShapeDtypeStruct((cols, size), bf16)] * 2
        + [jax.ShapeDtypeStruct((size, size), f32)],
        scratch_shapes=[pltpu.VMEM((size, size), bf16)] * 2,
        compiler_params=params(),
        cost_estimate=cost(
            2 * (9 * size**3 + 3 * size * cols * (size + n)), size * cols * 12
        ),
        name="prepare",
    )(left_param, weight, *rotations)


def grads_kernel(pieces, grad_pieces, has_prev, place, offsets, *refs):
    tokens = refs[:pieces]
    grads = refs[pieces : pieces + grad_pieces]
    m_h, m_l, v_h, v_l, *rest = refs[pieces + grad_pieces :]
    if has_prev:
        prev, rest = rest[0], rest[1:]
    left, right, peak, gathered, sems = rest
    span = tokens[0].shape[1]
    step = pl.program_id(0)

    @pl.when(step == 0)
    def _():
        copies = [
            pltpu.make_async_copy(
                tokens[k].at[pl.ds(place * gathered.shape[0], gathered.shape[0]), :],
                gathered.at[:, pl.ds(pl.multiple_of(offsets[k], span), span)],
                sems.at[k],
            )
            for k in range(pieces)
        ]
        for copy in copies:
            copy.start()
        for copy in copies:
            copy.wait()

    depth = grads[0].shape[0]
    value = None
    for k, grad in enumerate(grads):
        part = jnp.dot(
            gathered[:, k * depth : (k + 1) * depth], grad[...], preferred_element_type=f32
        )
        value = part if value is None else value + part
    halves = split(value)
    part = mul(halves, (m_h[...], m_l[...]), ((1,), (1,)))

    @pl.when(step == 0)
    def _():
        left[...] = part

    @pl.when(step != 0)
    def _():
        left[...] += part

    @pl.when(step == pl.num_programs(0) - 1)
    def _():
        peak[...] = jnp.full(peak.shape, jnp.max(jnp.abs(left[...])), f32)

    n = right.shape[-1]
    for b in range(right.shape[0]):
        cut = slice(b * n, (b + 1) * n)
        block = mul(
            (v_h[cut, :], v_l[cut, :]), (halves[0][:, cut], halves[1][:, cut])
        )
        right[b] = prev[b] + block if has_prev else block


def gradients(offsets, tokens, place, grads, prepared, prev, n, tile):
    size = prepared[0].shape[0]
    depth, cols = grads[0].shape
    total = depth * len(grads)
    pieces = len(tokens)
    wide = pl.BlockSpec((size, tile), lambda j, *_: (0, j))
    tall = pl.BlockSpec((tile, size), lambda j, *_: (j, 0))
    right_spec = pl.BlockSpec((tile // n, n, n), lambda j, *_: (j, 0, 0))
    more = [] if prev is None else [prev]
    return pl.pallas_call(
        functools.partial(grads_kernel, pieces, len(grads), prev is not None, place),
        grid_spec=pltpu.PrefetchScalarGridSpec(
            num_scalar_prefetch=1,
            grid=(cols // tile,),
            in_specs=[pl.BlockSpec(memory_space=pl.ANY)] * pieces
            + [pl.BlockSpec((depth, tile), lambda j, *_: (0, j))] * len(grads)
            + [wide, wide, tall, tall]
            + [right_spec] * len(more),
            out_specs=[
                pl.BlockSpec((size, size), lambda j, *_: (0, 0)),
                right_spec,
                pl.BlockSpec((8, 128), lambda j, *_: (0, 0)),
            ],
            scratch_shapes=[
                pltpu.VMEM((size, total), bf16),
                pltpu.SemaphoreType.DMA((pieces,)),
            ],
        ),
        out_shape=[
            jax.ShapeDtypeStruct((size, size), f32),
            jax.ShapeDtypeStruct((cols // n, n, n), f32),
            jax.ShapeDtypeStruct((8, 128), f32),
        ],
        compiler_params=params(),
        cost_estimate=cost(
            2 * size * cols * (total + 3 * (size + n)), total * cols * 2 + size * cols * 8
        ),
        name="gradients",
    )(offsets, *tokens, *grads, *prepared, *more)


def powers_kernel(many, param, *outs):
    skews = [-skew_of(param[b]) for b in range(many)]
    halves = [split(s) for s in skews]
    second = [mul(h, h) for h in halves]
    third = [mul(h, split(p)) for h, p in zip(halves, second)]
    unit = eye(param.shape[-1])
    for b in range(many):
        tail = unit / 6 + skews[b] / 24 + second[b] / 120 + third[b] / 720
        for k, value in enumerate((skews[b], second[b], third[b], tail)):
            outs[2 * k][b], outs[2 * k + 1][b] = split(value)


def powers(param):
    count, n, _ = param.shape
    many = max(1, math.gcd(count, 1024 // n))
    block = pl.BlockSpec((many, n, n), lambda i: (i, 0, 0))
    return pl.pallas_call(
        functools.partial(powers_kernel, many),
        grid=(count // many,),
        in_specs=[block],
        out_specs=[block] * 8,
        out_shape=[jax.ShapeDtypeStruct((count, n, n), bf16)] * 8,
        compiler_params=params(),
        cost_estimate=cost(count * 6 * n**3, count * n * n * 20),
        name="powers",
    )(param)


def adjoint_kernel(many, grad, *refs):
    *power_refs, out = refs
    sets = [
        [(power_refs[2 * k][b], power_refs[2 * k + 1][b]) for k in range(4)] for b in range(many)
    ]
    grads = [grad[b] for b in range(many)]
    halves = [split(g) for g in grads]
    d_second = [mul(h, s[0]) + mul(s[0], h) for h, s in zip(halves, sets)]
    d_third = [mul(split(d), s[0]) + mul(s[1], h) for d, h, s in zip(d_second, halves, sets)]
    n = grad.shape[-1]
    scale = 0.5 / math.sqrt(n)
    for b in range(many):
        d_tail = grads[b] / 24 + d_second[b] / 120 + d_third[b] / 720
        accum = (
            grads[b]
            + d_second[b] / 2
            + mul(split(d_third[b]), sets[b][3])
            + mul(sets[b][2], split(d_tail))
        )
        skewed = scale * (accum - accum.T)
        mean = jnp.sum(skewed * skewed, keepdims=True) * (1.0 / (n * n))
        skewed = skewed / jnp.sqrt(mean + epsilon)
        out[b, :, : n // 2], out[b, :, n // 2 :] = pack(skewed)


def directions(grad, power_list):
    count, n, _ = grad.shape
    many = max(1, math.gcd(count, 512 // n))
    block = pl.BlockSpec((many, n, n), lambda i: (i, 0, 0))
    return pl.pallas_call(
        functools.partial(adjoint_kernel, many),
        grid=(count // many,),
        in_specs=[block] * 9,
        out_specs=pl.BlockSpec((many, n // 2, n), lambda i: (i, 0, 0)),
        out_shape=jax.ShapeDtypeStruct((count, n // 2, n), f32),
        compiler_params=params(),
        cost_estimate=cost(count * 18 * n**3, count * n * n * 22),
        name="directions",
    )(grad, *power_list)


def turn_kernel(weight, rot_h, rot_l, out_h, out_l):
    halves = split(weight[...])
    n = rot_h.shape[-1]
    for b in range(rot_h.shape[0]):
        cut = slice(b * n, (b + 1) * n)
        out_h[:, cut], out_l[:, cut] = split(
            mul((halves[0][:, cut], halves[1][:, cut]), (rot_h[b], rot_l[b]))
        )


def turn_right(weight, rotations, high, tile):
    rows, cols = weight.shape
    n = rotations[0].shape[-1]
    rot_spec = pl.BlockSpec((tile // n, n, n), lambda j, i: (j, 0, 0))
    spec = pl.BlockSpec((high, tile), lambda j, i: (i, j))
    return pl.pallas_call(
        turn_kernel,
        grid=(cols // tile, rows // high),
        in_specs=[spec, rot_spec, rot_spec],
        out_specs=[spec, spec],
        out_shape=[jax.ShapeDtypeStruct((rows, cols), bf16)] * 2,
        compiler_params=params(2),
        cost_estimate=cost(3 * rows * cols * n, rows * cols * 8),
        name="turn_right",
    )(weight, *rotations)


def left_kernel(many, order, param, skew, packed, new, high, low):
    base = pl.program_id(0) * many
    size = param.shape[-1]
    skews = []
    for b in range(many):
        step = unpack(packed[order[base + b]])
        new[b] = param[b] - step_rate * step
        skews.append(skew[b] - (step_rate / math.sqrt(size)) * step)
    for b, value in enumerate(exponentials(skews)):
        high[b], low[b] = split(value)


def left_rotations(order, param, skews, packed):
    count, size, _ = param.shape
    many = math.gcd(count, 2)
    block = pl.BlockSpec((many, size, size), lambda i, o: (i, 0, 0))
    half = jax.ShapeDtypeStruct((count, size, size), bf16)
    return pl.pallas_call(
        functools.partial(left_kernel, many),
        grid_spec=pltpu.PrefetchScalarGridSpec(
            num_scalar_prefetch=1,
            grid=(count // many,),
            in_specs=[block, block, pl.BlockSpec(packed.shape, lambda i, o: (0, 0, 0))],
            out_specs=[block] * 3,
        ),
        out_shape=[jax.ShapeDtypeStruct((count, size, size), f32), half, half],
        compiler_params=params(),
        cost_estimate=cost(count * 9 * size**3, count * size * size * 14),
        name="left_rotations",
    )(order, param, skews, packed)


def final_kernel(rot_h, rot_l, turned_h, turned_l, out):
    out[...] = mul((rot_h[0], rot_l[0]), (turned_h[...], turned_l[...]))


def finish(rotations, turned, tile):
    count, size, _ = rotations[0].shape
    rows, cols = turned[0].shape
    wide = pl.BlockSpec((size, tile), lambda i, j: (i, j))
    square = pl.BlockSpec((1, size, size), lambda i, j: (i, 0, 0))
    return pl.pallas_call(
        final_kernel,
        grid=(count, cols // tile),
        in_specs=[square, square, wide, wide],
        out_specs=wide,
        out_shape=jax.ShapeDtypeStruct((rows, cols), f32),
        compiler_params=params(2),
        cost_estimate=cost(3 * rows * cols * size, rows * cols * 8),
        name="finish",
    )(*rotations, *turned)


def swap(value, axis):
    count = lax.axis_size(axis)
    return lax.ppermute(value, axis, [(d, d ^ 1) for d in range(count)])


def shift(value, axis, by=1):
    count = lax.axis_size(axis)
    return lax.ppermute(value, axis, [(d, (d + 2 * by) % count) for d in range(count)])


def pick(value, index, axis=0):
    return lax.dynamic_index_in_dim(value, index, axis, keepdims=False)


def gather_pieces(value, axis, kernels=()):
    count = lax.axis_size(axis)
    me = lax.axis_index(axis)
    pieces, sources = [], []
    held = value
    for hop in range(count // 2):
        if hop:
            held = shift(held, axis)
            if kernels:
                held = after(held, kernels[min(len(kernels) - 1, hop + 1)])
        source = (me - 2 * hop + count) % count
        pieces += [held, swap(held, axis)]
        sources += [source, source ^ 1]
    return pieces, sources


def sum_over_groups(parts, axis):
    groups = lax.axis_size(axis) // 2
    mine = lax.axis_index(axis) // 2
    total = pick(parts, mine)
    for by in range(1, groups):
        total = total + shift(pick(parts, (mine + by) % groups), axis, by)
    return total


top = 30000.0


def squared(value, order):
    return (value * jnp.abs(value) * (60000.0 / (0.5 * order**2))).astype(jnp.float16)


def rooted(sent, order):
    value = sent.astype(f32)
    return jnp.sign(value) * jnp.sqrt(jnp.abs(value) * ((0.5 * order**2) / 60000.0))


def after(value, *others):
    return lax.optimization_barrier((value, *others))[0]


def body(tokens, grad_out, base_weight, left_param, right_param):
    col_count = lax.axis_size("col")
    row_count = lax.axis_size("row")
    col = lax.axis_index("col")
    row = lax.axis_index("row")
    left_count, size, _ = left_param.shape
    right_count, n, _ = right_param.shape
    rows, cols = base_weight.shape
    tile = math.gcd(cols, 512)
    groups = col_count // 2
    left_split = left_count % groups == 0
    right_split = right_count % row_count == 0

    waves = math.gcd(left_count, 2)
    high = rows // waves
    turned_tokens = tokens.T
    rotations = right_rotations(right_param)
    kernels = []
    prepared, skews = [], []

    def prepare_next(*held_back):
        i = len(prepared)
        param = after(left_param, *held_back) if held_back else left_param
        *made, skew = prepare(i, param, base_weight, rotations, tile)
        prepared.append(made)
        skews.append(skew)
        kernels.append(skew)

    right_part = None
    sent_parts, left_parts, peaks = [], [], []

    def gradients_next(*held_back):
        nonlocal right_part
        i = len(left_parts)
        made = lax.optimization_barrier((*prepared[i], *held_back))[:4]
        left_part, right_part, peak = gradients(
            offsets,
            pieces[i * waves // left_count],
            i % (left_count // waves),
            grads,
            made,
            right_part,
            n,
            tile,
        )
        left_parts.append(left_part)
        peaks.append(peak)
        kernels.append(left_part)
        if left_split:
            shaped = left_part.reshape(2, size // 2, size)
            sent_parts.append(pick(shaped, 1 - col % 2))

    grads, grad_sources = [], []
    me = lax.axis_index("col")
    sources = []
    for hop in range(groups):
        source = (me - 2 * hop + col_count) % col_count
        sources += [source, source ^ 1]
    if left_split:
        left_own = left_count // groups
        own_left = lax.dynamic_slice_in_dim(left_param, (col // 2) * left_own, left_own, 0)
    else:
        own_left = left_param
    if right_split:
        right_own = right_count // row_count
        own_right = lax.dynamic_slice_in_dim(right_param, row * right_own, right_own, 0)
    else:
        own_right = right_param

    pieces = []
    swapped = []
    offsets = None

    def gather_grads():
        nonlocal offsets
        grads[:], grad_sources[:] = gather_pieces(grad_out, "row", kernels)
        span = grad_out.shape[0]
        place = jnp.zeros((row_count,), jnp.int32)
        for k, source in enumerate(grad_sources):
            place = jnp.where(jnp.arange(row_count) == source, k, place)
        first = jnp.stack(sources).astype(jnp.int32) * tokens.shape[0]
        offsets = place[first // span] * span + first % span

    for wave in range(waves):
        held = turned_tokens[wave * high : (wave + 1) * high]
        if kernels:
            held = after(held, moved)
        here = []
        pieces.append(here)
        for hop in range(groups):
            if hop:
                held = moved = shift(held, "col")
                if kernels:
                    held = after(held, kernels[-1])
            ties = [held] + swapped[-1:] if hop or wave else []
            swapped.append(swap(held, "col"))
            here += [held, swapped[-1]]
            if wave and not hop:
                continue
            if len(prepared) < left_count:
                prepare_next(*ties)
            elif len(left_parts) < left_count // waves * wave:
                if not grads:
                    gather_grads()
                gradients_next(*ties)
    while len(prepared) < left_count:
        prepare_next()
    if not grads:
        gather_grads()
    while len(left_parts) < left_count // waves * (waves - 1):
        gradients_next()
    own_left, own_right, skews = lax.optimization_barrier(
        (own_left, own_right, jnp.stack(skews), kernels[-1])
    )[:3]
    left_powers = powers(own_left)
    right_powers = powers(own_right)
    ties = [left_powers[0], right_powers[0], skews]
    while len(left_parts) < left_count:
        gradients_next(*ties)
        ties = sent_parts[-1:]

    left_halves = []
    if left_split:
        for left_part, sent in zip(left_parts, sent_parts):
            shaped = left_part.reshape(2, size // 2, size)
            left_halves.append(pick(shaped, col % 2) + swap(sent, "col"))

    if right_split:
        outer = row_count // 2
        shaped = right_part.reshape(outer, 2, right_own, n, n)
        mine = pick(shaped, row % 2, 1) + swap(pick(shaped, 1 - row % 2, 1), "row")
        right_grad = sum_over_groups(mine, "row")
    else:
        right_grad = lax.psum(right_part, "row")

    right_packed = directions(right_grad, right_powers)
    if right_split:
        held, sources = gather_pieces(right_packed, "row")
        packed_all = jnp.concatenate(held, 0)
        place = jnp.zeros((row_count,), jnp.int32)
        for k, source in enumerate(sources):
            place = place + jnp.where(jnp.arange(row_count) == source, k, 0)
        right_order = (
            place[:, None] * right_own + jnp.arange(right_own)[None, :]
        ).reshape(-1).astype(jnp.int32)
    else:
        packed_all = right_packed
        right_order = jnp.arange(right_count, dtype=jnp.int32)

    if left_split:
        halves = jnp.stack(left_halves).reshape(groups, left_own, size // 2, size)
        group = col // 2
        most = functools.reduce(jnp.maximum, peaks)
        most = jnp.maximum(most + swap(most, "col"), 1e-30)
        mine = pick(halves, group)
        for by in range(1, groups):
            sent = pick(halves, (group + by) % groups) * (top / most[0, 0])
            theirs = shift(most, "col", by)[0, 0] / top
            mine = mine + shift(sent.astype(jnp.float16), "col", by).astype(f32) * theirs
        other = swap(mine, "col")
        first = jnp.where(col % 2 == 0, mine, other)
        last = jnp.where(col % 2 == 0, other, mine)
        left_grad = jnp.concatenate([first, last], 1)
    else:
        left_grad = lax.psum(jnp.stack(left_parts), "col")

    left_packed = directions(after(left_grad, right_packed), left_powers)
    if left_split:
        sent = squared(left_packed, size)
        held = [sent] + [shift(sent, "col", by) for by in range(1, groups)]
        block = jnp.arange(left_count)
        back = (group - block // left_own + groups) % groups
        left_order = (back * left_own + block % left_own).astype(jnp.int32)
        packed_all = after(packed_all, left_packed)
    else:
        left_all = left_packed
        left_order = jnp.arange(left_count, dtype=jnp.int32)
    new_right, *new_rotations = right_rotations(right_param, packed_all, right_order)
    turned = turn_right(base_weight, new_rotations, math.gcd(rows, 512), math.gcd(cols, 2048))
    if left_split:
        held = lax.optimization_barrier((*held, turned[0]))[:-1]
        left_all = rooted(jnp.concatenate(held, 0), size)
    new_left, *left_rots = left_rotations(left_order, left_param, skews, left_all)
    rotated_weight = finish(left_rots, turned, math.gcd(cols, 2048))
    return (rotated_weight, new_left, new_right)


def solution(mesh):
    return jax.shard_map(
        body,
        mesh=mesh,
        in_specs=(
            P("col", "row"),
            P("row", "col"),
            P("row", "col"),
            P("row", None, None),
            P("col", None, None),
        ),
        out_specs=(P("row", "col"), P("row", None, None), P("col", None, None)),
        check_vma=False,
    )
```

```python
import functools
import math

import jax
import jax.numpy as jnp
from jax import lax
from jax.experimental import pallas as pl
from jax.experimental.pallas import tpu as pltpu
from jax.sharding import PartitionSpec as P

step_rate = 0.3
epsilon = 1e-06
f32 = jnp.float32
bf16 = jnp.bfloat16
VMEM_BYTES = 52 * 1024 * 1024


def params(count=1):
    return pltpu.CompilerParams(
        dimension_semantics=("arbitrary",) * count, vmem_limit_bytes=VMEM_BYTES
    )


def cost(macs, moved):
    return pl.CostEstimate(flops=int(2 * macs), bytes_accessed=int(moved), transcendentals=0)


def split(value):
    high = value.astype(bf16)
    return high, (value - high.astype(f32)).astype(bf16)


def mul(first, second, dims=((1,), (0,))):
    def one(a, b):
        return lax.dot_general(a, b, (dims, ((), ())), preferred_element_type=f32)

    return one(first[0], second[0]) + (one(first[0], second[1]) + one(first[1], second[0]))


def eye(order):
    row = lax.broadcasted_iota(jnp.int32, (order, order), 0)
    col = lax.broadcasted_iota(jnp.int32, (order, order), 1)
    return jnp.where(row == col, 1.0, 0.0).astype(f32)


def skew_of(param):
    return (0.5 / math.sqrt(param.shape[-1])) * (param - param.T)


def exponentials(skews):
    halves = [split(s) for s in skews]
    second = [mul(h, h) for h in halves]
    third = [mul(h, split(p)) for h, p in zip(halves, second)]
    unit = eye(skews[0].shape[-1])
    tails = [
        split(unit / 6 + s / 24 + p / 120 + c / 720) for s, p, c in zip(skews, second, third)
    ]
    return [
        unit + s + p / 2 + mul(split(c), t)
        for s, p, c, t in zip(skews, second, third, tails)
    ]


def pack(skew):
    half = skew.shape[-1] // 2
    row = lax.broadcasted_iota(jnp.int32, (half, half), 0)
    col = lax.broadcasted_iota(jnp.int32, (half, half), 1)
    mixed = jnp.where(row < col, skew[:half, :half], skew[half:, half:])
    return mixed, skew[:half, half:]


def unpack(packed):
    half = packed.shape[0]
    row = lax.broadcasted_iota(jnp.int32, (half, half), 0)
    col = lax.broadcasted_iota(jnp.int32, (half, half), 1)
    mixed = packed[:, :half]
    upper = packed[:, half:]
    first = jnp.where(row < col, mixed, 0.0)
    last = jnp.where(row > col, mixed, 0.0)
    return jnp.concatenate(
        [
            jnp.concatenate([first - first.T, upper], 1),
            jnp.concatenate([-upper.T, last - last.T], 1),
        ],
        0,
    )


def right_kernel(many, updates, *refs):
    if updates:
        order, param, packed, new, high, low = refs
        base = pl.program_id(0) * many
        values = []
        for b in range(many):
            value = param[b] - step_rate * unpack(packed[order[base + b]])
            new[b] = value
            values.append(value)
    else:
        param, high, low = refs
        values = [param[b] for b in range(many)]
    for b, value in enumerate(exponentials([skew_of(v) for v in values])):
        high[b], low[b] = split(value)


def right_rotations(param, packed=None, order=None):
    count, n, _ = param.shape
    many = math.gcd(count, 4)
    updates = packed is not None
    block = pl.BlockSpec((many, n, n), lambda i, *_: (i, 0, 0))
    half = jax.ShapeDtypeStruct((count, n, n), bf16)
    in_specs, outs = [block], [half, half]
    if updates:
        in_specs.append(pl.BlockSpec(packed.shape, lambda i, *_: (0, 0, 0)))
        outs.insert(0, jax.ShapeDtypeStruct((count, n, n), f32))
    call = pl.pallas_call(
        functools.partial(right_kernel, many, updates),
        grid_spec=pltpu.PrefetchScalarGridSpec(
            num_scalar_prefetch=1 if updates else 0,
            grid=(count // many,),
            in_specs=in_specs,
            out_specs=[block] * len(outs),
        ),
        out_shape=outs,
        compiler_params=params(),
        cost_estimate=cost(count * 9 * n**3, count * n * n * 12),
        name="right_rotations",
    )
    return call(order, param, packed) if updates else call(param)


def prep_kernel(param, weight, rot_h, rot_l, m_h, m_l, v_h, v_l, skew, left_h, left_l):
    @pl.when(pl.program_id(0) == 0)
    def _():
        value = skew_of(param[0])
        skew[...] = value
        (rotation,) = exponentials([value])
        left_h[...], left_l[...] = split(rotation)

    halves = split(weight[...])
    n = rot_h.shape[-1]
    for b in range(rot_h.shape[0]):
        cut = slice(b * n, (b + 1) * n)
        value = mul((halves[0][:, cut], halves[1][:, cut]), (rot_h[b], rot_l[b]))
        m_h[:, cut], m_l[:, cut] = split(value)
    high, low = split(mul((left_h[...], left_l[...]), halves))
    v_h[...] = high.T
    v_l[...] = low.T


def prepare(i, left_param, weight, rotations, tile):
    size = left_param.shape[-1]
    cols = weight.shape[1]
    n = rotations[0].shape[-1]
    rot_spec = pl.BlockSpec((tile // n, n, n), lambda j: (j, 0, 0))
    wide = pl.BlockSpec((size, tile), lambda j: (0, j))
    tall = pl.BlockSpec((tile, size), lambda j: (j, 0))
    return pl.pallas_call(
        prep_kernel,
        grid=(cols // tile,),
        in_specs=[
            pl.BlockSpec((1, size, size), lambda j: (i, 0, 0)),
            pl.BlockSpec((size, tile), lambda j: (i, j)),
            rot_spec,
            rot_spec,
        ],
        out_specs=[
            wide,
            wide,
            tall,
            tall,
            pl.BlockSpec((size, size), lambda j: (0, 0)),
        ],
        out_shape=[jax.ShapeDtypeStruct((size, cols), bf16)] * 2
        + [jax.ShapeDtypeStruct((cols, size), bf16)] * 2
        + [jax.ShapeDtypeStruct((size, size), f32)],
        scratch_shapes=[pltpu.VMEM((size, size), bf16)] * 2,
        compiler_params=params(),
        cost_estimate=cost(
            (9 * size**3 + 3 * size * cols * (size + n)) // 2, size * cols * 2
        ),
        name="prepare",
    )(left_param, weight, *rotations)


def grads_kernel(pieces, grad_pieces, has_prev, starts, offsets, *refs):
    tokens = refs[:pieces]
    grads = refs[pieces : pieces + grad_pieces]
    m_h, m_l, v_h, v_l, *rest = refs[pieces + grad_pieces :]
    if has_prev:
        prev, rest = rest[0], rest[1:]
    left, right, peak, gathered, sems = rest
    span = tokens[0].shape[1]
    step = pl.program_id(0)

    @pl.when(step == 0)
    def _():
        copies = [
            pltpu.make_async_copy(
                tokens[k].at[pl.ds(starts[k], gathered.shape[0]), :],
                gathered.at[:, pl.ds(pl.multiple_of(offsets[k], span), span)],
                sems.at[k],
            )
            for k in range(pieces)
        ]
        for copy in copies:
            copy.start()
        for copy in copies:
            copy.wait()

    depth = grads[0].shape[0]
    value = None
    for k, grad in enumerate(grads):
        part = jnp.dot(
            gathered[:, k * depth : (k + 1) * depth], grad[...], preferred_element_type=f32
        )
        value = part if value is None else value + part
    halves = split(value)
    part = mul(halves, (m_h[...], m_l[...]), ((1,), (1,)))

    @pl.when(step == 0)
    def _():
        left[...] = part

    @pl.when(step != 0)
    def _():
        left[...] += part

    @pl.when(step == pl.num_programs(0) - 1)
    def _():
        peak[...] = jnp.full(peak.shape, jnp.max(jnp.abs(left[...])), f32)

    n = right.shape[-1]
    for b in range(right.shape[0]):
        cut = slice(b * n, (b + 1) * n)
        block = mul(
            (v_h[cut, :], v_l[cut, :]), (halves[0][:, cut], halves[1][:, cut])
        )
        right[b] = prev[b] + block if has_prev else block


def gradients(offsets, tokens, starts, grads, prepared, prev, n, tile):
    size = prepared[0].shape[0]
    depth, cols = grads[0].shape
    total = depth * len(grads)
    pieces = len(tokens)
    wide = pl.BlockSpec((size, tile), lambda j, *_: (0, j))
    tall = pl.BlockSpec((tile, size), lambda j, *_: (j, 0))
    right_spec = pl.BlockSpec((tile // n, n, n), lambda j, *_: (j, 0, 0))
    more = [] if prev is None else [prev]
    return pl.pallas_call(
        functools.partial(grads_kernel, pieces, len(grads), prev is not None, tuple(starts)),
        grid_spec=pltpu.PrefetchScalarGridSpec(
            num_scalar_prefetch=1,
            grid=(cols // tile,),
            in_specs=[pl.BlockSpec(memory_space=pl.ANY)] * pieces
            + [pl.BlockSpec((depth, tile), lambda j, *_: (0, j))] * len(grads)
            + [wide, wide, tall, tall]
            + [right_spec] * len(more),
            out_specs=[
                pl.BlockSpec((size, size), lambda j, *_: (0, 0)),
                right_spec,
                pl.BlockSpec((8, 128), lambda j, *_: (0, 0)),
            ],
            scratch_shapes=[
                pltpu.VMEM((size, total), bf16),
                pltpu.SemaphoreType.DMA((pieces,)),
            ],
        ),
        out_shape=[
            jax.ShapeDtypeStruct((size, size), f32),
            jax.ShapeDtypeStruct((cols // n, n, n), f32),
            jax.ShapeDtypeStruct((8, 128), f32),
        ],
        compiler_params=params(),
        cost_estimate=cost(
            size * cols * (total + 3 * (size + n)) // 2, total * cols * 2
        ),
        name="gradients",
    )(offsets, *tokens, *grads, *prepared, *more)


def powers_kernel(many, param, *outs):
    skews = [-skew_of(param[b]) for b in range(many)]
    halves = [split(s) for s in skews]
    second = [mul(h, h) for h in halves]
    third = [mul(h, split(p)) for h, p in zip(halves, second)]
    unit = eye(param.shape[-1])
    for b in range(many):
        tail = unit / 6 + skews[b] / 24 + second[b] / 120 + third[b] / 720
        for k, value in enumerate((skews[b], second[b], third[b], tail)):
            outs[2 * k][b], outs[2 * k + 1][b] = split(value)


def powers(param):
    count, n, _ = param.shape
    many = max(1, math.gcd(count, 1024 // n))
    block = pl.BlockSpec((many, n, n), lambda i: (i, 0, 0))
    return pl.pallas_call(
        functools.partial(powers_kernel, many),
        grid=(count // many,),
        in_specs=[block],
        out_specs=[block] * 8,
        out_shape=[jax.ShapeDtypeStruct((count, n, n), bf16)] * 8,
        compiler_params=params(),
        cost_estimate=cost(count * 6 * n**3, count * n * n * 20),
        name="powers",
    )(param)


def adjoint_kernel(many, grad, *refs):
    *power_refs, out = refs
    sets = [
        [(power_refs[2 * k][b], power_refs[2 * k + 1][b]) for k in range(4)] for b in range(many)
    ]
    grads = [grad[b] for b in range(many)]
    halves = [split(g) for g in grads]
    d_second = [mul(h, s[0]) + mul(s[0], h) for h, s in zip(halves, sets)]
    d_third = [mul(split(d), s[0]) + mul(s[1], h) for d, h, s in zip(d_second, halves, sets)]
    n = grad.shape[-1]
    scale = 0.5 / math.sqrt(n)
    for b in range(many):
        d_tail = grads[b] / 24 + d_second[b] / 120 + d_third[b] / 720
        accum = (
            grads[b]
            + d_second[b] / 2
            + mul(split(d_third[b]), sets[b][3])
            + mul(sets[b][2], split(d_tail))
        )
        skewed = scale * (accum - accum.T)
        mean = jnp.sum(skewed * skewed, keepdims=True) * (1.0 / (n * n))
        skewed = skewed / jnp.sqrt(mean + epsilon)
        out[b, :, : n // 2], out[b, :, n // 2 :] = pack(skewed)


def directions(grad, power_list):
    count, n, _ = grad.shape
    many = max(1, math.gcd(count, 512 // n))
    block = pl.BlockSpec((many, n, n), lambda i: (i, 0, 0))
    return pl.pallas_call(
        functools.partial(adjoint_kernel, many),
        grid=(count // many,),
        in_specs=[block] * 9,
        out_specs=pl.BlockSpec((many, n // 2, n), lambda i: (i, 0, 0)),
        out_shape=jax.ShapeDtypeStruct((count, n // 2, n), f32),
        compiler_params=params(),
        cost_estimate=cost(count * 18 * n**3, count * n * n * 22),
        name="directions",
    )(grad, *power_list)


def turn_kernel(weight, rot_h, rot_l, out_h, out_l):
    halves = split(weight[...])
    n = rot_h.shape[-1]
    for b in range(rot_h.shape[0]):
        cut = slice(b * n, (b + 1) * n)
        out_h[:, cut], out_l[:, cut] = split(
            mul((halves[0][:, cut], halves[1][:, cut]), (rot_h[b], rot_l[b]))
        )


def turn_right(weight, rotations, high, tile):
    rows, cols = weight.shape
    n = rotations[0].shape[-1]
    rot_spec = pl.BlockSpec((tile // n, n, n), lambda j, i: (j, 0, 0))
    spec = pl.BlockSpec((high, tile), lambda j, i: (i, j))
    return pl.pallas_call(
        turn_kernel,
        grid=(cols // tile, rows // high),
        in_specs=[spec, rot_spec, rot_spec],
        out_specs=[spec, spec],
        out_shape=[jax.ShapeDtypeStruct((rows, cols), bf16)] * 2,
        compiler_params=params(2),
        cost_estimate=cost(3 * rows * cols * n, rows * cols * 8),
        name="turn_right",
    )(weight, *rotations)


def left_kernel(many, order, param, skew, packed, new, high, low):
    base = pl.program_id(0) * many
    size = param.shape[-1]
    skews = []
    for b in range(many):
        step = unpack(packed[order[base + b]])
        new[b] = param[b] - step_rate * step
        skews.append(skew[b] - (step_rate / math.sqrt(size)) * step)
    for b, value in enumerate(exponentials(skews)):
        high[b], low[b] = split(value)


def left_rotations(order, param, skews, packed):
    count, size, _ = param.shape
    many = math.gcd(count, 2)
    block = pl.BlockSpec((many, size, size), lambda i, o: (i, 0, 0))
    half = jax.ShapeDtypeStruct((count, size, size), bf16)
    return pl.pallas_call(
        functools.partial(left_kernel, many),
        grid_spec=pltpu.PrefetchScalarGridSpec(
            num_scalar_prefetch=1,
            grid=(count // many,),
            in_specs=[block, block, pl.BlockSpec(packed.shape, lambda i, o: (0, 0, 0))],
            out_specs=[block] * 3,
        ),
        out_shape=[jax.ShapeDtypeStruct((count, size, size), f32), half, half],
        compiler_params=params(),
        cost_estimate=cost(count * 9 * size**3, count * size * size * 14),
        name="left_rotations",
    )(order, param, skews, packed)


def final_kernel(rot_h, rot_l, turned_h, turned_l, out):
    out[...] = mul((rot_h[0], rot_l[0]), (turned_h[...], turned_l[...]))


def finish(rotations, turned, tile):
    count, size, _ = rotations[0].shape
    rows, cols = turned[0].shape
    wide = pl.BlockSpec((size, tile), lambda i, j: (i, j))
    square = pl.BlockSpec((1, size, size), lambda i, j: (i, 0, 0))
    return pl.pallas_call(
        final_kernel,
        grid=(count, cols // tile),
        in_specs=[square, square, wide, wide],
        out_specs=wide,
        out_shape=jax.ShapeDtypeStruct((rows, cols), f32),
        compiler_params=params(2),
        cost_estimate=cost(3 * rows * cols * size, rows * cols * 8),
        name="finish",
    )(*rotations, *turned)


def swap(value, axis):
    count = lax.axis_size(axis)
    return lax.ppermute(value, axis, [(d, d ^ 1) for d in range(count)])


def shift(value, axis, by=1):
    count = lax.axis_size(axis)
    return lax.ppermute(value, axis, [(d, (d + 2 * by) % count) for d in range(count)])


def pick(value, index, axis=0):
    return lax.dynamic_index_in_dim(value, index, axis, keepdims=False)


def gather_pieces(value, axis, kernels=()):
    count = lax.axis_size(axis)
    me = lax.axis_index(axis)
    pieces, sources = [], []
    held = value
    for hop in range(count // 2):
        if hop:
            held = shift(held, axis)
            if kernels:
                held = after(held, kernels[min(len(kernels) - 1, hop + 1)])
        source = (me - 2 * hop + count) % count
        pieces += [held, swap(held, axis)]
        sources += [source, source ^ 1]
    return pieces, sources


def sum_over_groups(parts, axis):
    groups = lax.axis_size(axis) // 2
    mine = lax.axis_index(axis) // 2
    total = pick(parts, mine)
    for by in range(1, groups):
        total = total + shift(pick(parts, (mine + by) % groups), axis, by)
    return total


top = 30000.0


def squared(value, order):
    return (value * jnp.abs(value) * (60000.0 / (0.5 * order**2))).astype(jnp.float16)


def rooted(sent, order):
    value = sent.astype(f32)
    return jnp.sign(value) * jnp.sqrt(jnp.abs(value) * ((0.5 * order**2) / 60000.0))


def after(value, *others):
    return lax.optimization_barrier((value, *others))[0]


def body(tokens, grad_out, base_weight, left_param, right_param):
    col_count = lax.axis_size("col")
    row_count = lax.axis_size("row")
    col = lax.axis_index("col")
    row = lax.axis_index("row")
    left_count, size, _ = left_param.shape
    right_count, n, _ = right_param.shape
    rows, cols = base_weight.shape
    tile = math.gcd(cols, 512)
    groups = col_count // 2
    left_split = left_count % groups == 0
    right_split = right_count % row_count == 0

    turned_tokens = tokens.T
    rotations = right_rotations(right_param)
    kernels = []
    prepared, skews = [], []

    def prepare_next(*held_back):
        i = len(prepared)
        param = after(left_param, *held_back) if held_back else left_param
        *made, skew = prepare(i, param, base_weight, rotations, tile)
        prepared.append(made)
        skews.append(skew)
        kernels.append(skew)

    right_part = None
    sent_parts, others, left_parts, peaks = [], [], [], []

    def gradients_next(*held_back):
        nonlocal right_part
        i = len(left_parts)
        made = lax.optimization_barrier((*prepared[i], *held_back))[:4]
        here = [(p[i * len(p) // left_count], i % (left_count // len(p)) * size) for p in pieces]
        left_part, right_part, peak = gradients(
            offsets,
            [p for p, _ in here],
            [start for _, start in here],
            grads,
            made,
            right_part,
            n,
            tile,
        )
        left_parts.append(left_part)
        peaks.append(peak)
        kernels.append(left_part)
        if left_split:
            shaped = left_part.reshape(2, size // 2, size)
            sent_parts.append(pick(shaped, 1 - col % 2))
            others.append(swap(sent_parts[-1], "col"))

    own_powers = []

    def powers_next(*ties):
        held = lax.optimization_barrier(
            (own_left, own_right, jnp.stack(skews), kernels[-1], *ties)
        )
        left_powers = powers(held[0])
        right_powers = powers(after(held[1], left_powers[0]))
        own_powers[:] = [left_powers, right_powers, held[2]]
        kernels.append(right_powers[0])

    grads, grad_sources = [], []
    me = lax.axis_index("col")
    sources = []
    for hop in range(groups):
        source = (me - 2 * hop + col_count) % col_count
        sources += [source, source ^ 1]
    if left_split:
        left_own = left_count // groups
        own_left = lax.dynamic_slice_in_dim(left_param, (col // 2) * left_own, left_own, 0)
    else:
        own_left = left_param
    if right_split:
        right_own = right_count // row_count
        own_right = lax.dynamic_slice_in_dim(right_param, row * right_own, right_own, 0)
    else:
        own_right = right_param

    pieces = []
    swapped = []
    offsets = None

    def gather_grads():
        nonlocal offsets
        grads[:], grad_sources[:] = gather_pieces(grad_out, "row", kernels)
        span = grad_out.shape[0]
        place = jnp.zeros((row_count,), jnp.int32)
        for k, source in enumerate(grad_sources):
            place = jnp.where(jnp.arange(row_count) == source, k, place)
        first = jnp.stack(sources).astype(jnp.int32) * tokens.shape[0]
        offsets = place[first // span] * span + first % span

    held = turned_tokens
    half = rows // 2
    for hop in range(groups):
        if hop:
            held = after(shift(held, "col"), kernels[-1])
        ties = [held] + swapped[-1:] if hop else []
        pieces.append((held,))
        if 0 < hop == groups - 1 and left_count % 2 == 0:
            behind = after(swapped[-1][half:], kernels[-1])
            pieces.append((swap(held[:half], "col"), shift(behind, "col")))
            powers_next(*ties)
        else:
            swapped.append(swap(held, "col"))
            pieces.append(swapped[-1:])
        while len(prepared) < left_count and hop >= (len(prepared) + 1) // 2:
            prepare_next(*ties)
    while len(prepared) < left_count:
        prepare_next()
    gather_grads()
    if not own_powers:
        powers_next()
    left_powers, right_powers, skews = own_powers
    ties = [left_powers[0]]
    while len(left_parts) < left_count:
        gradients_next(*ties)
        ties = sent_parts[-1:] + others[-2:-1]

    left_halves = []
    if left_split:
        for left_part, other in zip(left_parts, others):
            shaped = left_part.reshape(2, size // 2, size)
            left_halves.append(pick(shaped, col % 2) + other)

    if right_split:
        outer = row_count // 2
        shaped = right_part.reshape(outer, 2, right_own, n, n)
        mine = pick(shaped, row % 2, 1) + swap(pick(shaped, 1 - row % 2, 1), "row")
        right_grad = sum_over_groups(mine, "row")
    else:
        right_grad = lax.psum(right_part, "row")

    right_packed = directions(right_grad, right_powers)
    if right_split:
        held, sources = gather_pieces(right_packed, "row")
        packed_all = jnp.concatenate(held, 0)
        place = jnp.zeros((row_count,), jnp.int32)
        for k, source in enumerate(sources):
            place = place + jnp.where(jnp.arange(row_count) == source, k, 0)
        right_order = (
            place[:, None] * right_own + jnp.arange(right_own)[None, :]
        ).reshape(-1).astype(jnp.int32)
    else:
        packed_all = right_packed
        right_order = jnp.arange(right_count, dtype=jnp.int32)

    if left_split:
        halves = jnp.stack(left_halves).reshape(groups, left_own, size // 2, size)
        group = col // 2
        most = functools.reduce(jnp.maximum, peaks)
        most = jnp.maximum(most + swap(most, "col"), 1e-30)
        mine = pick(halves, group)
        for by in range(1, groups):
            sent = pick(halves, (group + by) % groups) * (top / most[0, 0])
            theirs = shift(most, "col", by)[0, 0] / top
            mine = mine + shift(sent.astype(jnp.float16), "col", by).astype(f32) * theirs
        other = swap(mine, "col")
        first = jnp.where(col % 2 == 0, mine, other)
        last = jnp.where(col % 2 == 0, other, mine)
        left_grad = jnp.concatenate([first, last], 1)
    else:
        left_grad = lax.psum(jnp.stack(left_parts), "col")

    left_packed = directions(after(left_grad, right_packed), left_powers)
    if left_split:
        sent = squared(left_packed, size)
        held = [sent] + [shift(sent, "col", by) for by in range(1, groups)]
        block = jnp.arange(left_count)
        back = (group - block // left_own + groups) % groups
        left_order = (back * left_own + block % left_own).astype(jnp.int32)
        packed_all = after(packed_all, left_packed)
    else:
        left_all = left_packed
        left_order = jnp.arange(left_count, dtype=jnp.int32)
    new_right, *new_rotations = right_rotations(right_param, packed_all, right_order)
    turned = turn_right(base_weight, new_rotations, math.gcd(rows, 512), math.gcd(cols, 2048))
    if left_split:
        held = lax.optimization_barrier((*held, turned[0]))[:-1]
        left_all = rooted(jnp.concatenate(held, 0), size)
    new_left, *left_rots = left_rotations(left_order, left_param, skews, left_all)
    rotated_weight = finish(left_rots, turned, math.gcd(cols, 2048))
    return (rotated_weight, new_left, new_right)


def solution(mesh):
    return jax.shard_map(
        body,
        mesh=mesh,
        in_specs=(
            P("col", "row"),
            P("row", "col"),
            P("row", "col"),
            P("row", None, None),
            P("col", None, None),
        ),
        out_specs=(P("row", "col"), P("row", None, None), P("col", None, None)),
        check_vma=False,
    )
```

```python
import functools
import math

import jax
import jax.numpy as jnp
from jax import lax
from jax.experimental import pallas as pl
from jax.experimental.pallas import tpu as pltpu
from jax.sharding import PartitionSpec as P

step_rate = 0.3
epsilon = 1e-06
f32 = jnp.float32
bf16 = jnp.bfloat16
VMEM_BYTES = 52 * 1024 * 1024


def params(count=1):
    return pltpu.CompilerParams(
        dimension_semantics=("arbitrary",) * count, vmem_limit_bytes=VMEM_BYTES
    )


def cost(macs, moved):
    return pl.CostEstimate(flops=int(2 * macs), bytes_accessed=int(moved), transcendentals=0)


def split(value):
    high = value.astype(bf16)
    return high, (value - high.astype(f32)).astype(bf16)


def mul(first, second, dims=((1,), (0,))):
    def one(a, b):
        return lax.dot_general(a, b, (dims, ((), ())), preferred_element_type=f32)

    return one(first[0], second[0]) + (one(first[0], second[1]) + one(first[1], second[0]))


def eye(order):
    row = lax.broadcasted_iota(jnp.int32, (order, order), 0)
    col = lax.broadcasted_iota(jnp.int32, (order, order), 1)
    return jnp.where(row == col, 1.0, 0.0).astype(f32)


def skew_of(param):
    return (0.5 / math.sqrt(param.shape[-1])) * (param - param.T)


def exponentials(skews):
    halves = [split(s) for s in skews]
    second = [mul(h, h) for h in halves]
    third = [mul(h, split(p)) for h, p in zip(halves, second)]
    unit = eye(skews[0].shape[-1])
    tails = [
        split(unit / 6 + s / 24 + p / 120 + c / 720) for s, p, c in zip(skews, second, third)
    ]
    return [
        unit + s + p / 2 + mul(split(c), t)
        for s, p, c, t in zip(skews, second, third, tails)
    ]


def pack(skew):
    half = skew.shape[-1] // 2
    row = lax.broadcasted_iota(jnp.int32, (half, half), 0)
    col = lax.broadcasted_iota(jnp.int32, (half, half), 1)
    mixed = jnp.where(row < col, skew[:half, :half], skew[half:, half:])
    return mixed, skew[:half, half:]


def unpack(packed):
    half = packed.shape[0]
    row = lax.broadcasted_iota(jnp.int32, (half, half), 0)
    col = lax.broadcasted_iota(jnp.int32, (half, half), 1)
    mixed = packed[:, :half]
    upper = packed[:, half:]
    first = jnp.where(row < col, mixed, 0.0)
    last = jnp.where(row > col, mixed, 0.0)
    return jnp.concatenate(
        [
            jnp.concatenate([first - first.T, upper], 1),
            jnp.concatenate([-upper.T, last - last.T], 1),
        ],
        0,
    )


def right_kernel(many, updates, *refs):
    if updates:
        order, param, packed, new, high, low = refs
        base = pl.program_id(0) * many
        values = []
        for b in range(many):
            value = param[b] - step_rate * unpack(packed[order[base + b]])
            new[b] = value
            values.append(value)
    else:
        param, high, low = refs
        values = [param[b] for b in range(many)]
    for b, value in enumerate(exponentials([skew_of(v) for v in values])):
        high[b], low[b] = split(value)


def right_rotations(param, packed=None, order=None):
    count, n, _ = param.shape
    many = math.gcd(count, 4)
    updates = packed is not None
    block = pl.BlockSpec((many, n, n), lambda i, *_: (i, 0, 0))
    half = jax.ShapeDtypeStruct((count, n, n), bf16)
    in_specs, outs = [block], [half, half]
    if updates:
        in_specs.append(pl.BlockSpec(packed.shape, lambda i, *_: (0, 0, 0)))
        outs.insert(0, jax.ShapeDtypeStruct((count, n, n), f32))
    call = pl.pallas_call(
        functools.partial(right_kernel, many, updates),
        grid_spec=pltpu.PrefetchScalarGridSpec(
            num_scalar_prefetch=1 if updates else 0,
            grid=(count // many,),
            in_specs=in_specs,
            out_specs=[block] * len(outs),
        ),
        out_shape=outs,
        compiler_params=params(),
        cost_estimate=cost(count * 9 * n**3, count * n * n * 12),
        name="right_rotations",
    )
    return call(order, param, packed) if updates else call(param)


def prep_kernel(param, weight, rot_h, rot_l, m_h, m_l, v_h, v_l, skew, left_h, left_l):
    @pl.when(pl.program_id(0) == 0)
    def _():
        value = skew_of(param[0])
        skew[...] = value
        (rotation,) = exponentials([value])
        left_h[...], left_l[...] = split(rotation)

    halves = split(weight[...])
    n = rot_h.shape[-1]
    for b in range(rot_h.shape[0]):
        cut = slice(b * n, (b + 1) * n)
        value = mul((halves[0][:, cut], halves[1][:, cut]), (rot_h[b], rot_l[b]))
        m_h[:, cut], m_l[:, cut] = split(value)
    high, low = split(mul((left_h[...], left_l[...]), halves))
    v_h[...] = high.T
    v_l[...] = low.T


def prepare(i, left_param, weight, rotations, tile):
    size = left_param.shape[-1]
    cols = weight.shape[1]
    n = rotations[0].shape[-1]
    rot_spec = pl.BlockSpec((tile // n, n, n), lambda j: (j, 0, 0))
    wide = pl.BlockSpec((size, tile), lambda j: (0, j))
    tall = pl.BlockSpec((tile, size), lambda j: (j, 0))
    return pl.pallas_call(
        prep_kernel,
        grid=(cols // tile,),
        in_specs=[
            pl.BlockSpec((1, size, size), lambda j: (i, 0, 0)),
            pl.BlockSpec((size, tile), lambda j: (i, j)),
            rot_spec,
            rot_spec,
        ],
        out_specs=[
            wide,
            wide,
            tall,
            tall,
            pl.BlockSpec((size, size), lambda j: (0, 0)),
        ],
        out_shape=[jax.ShapeDtypeStruct((size, cols), bf16)] * 2
        + [jax.ShapeDtypeStruct((cols, size), bf16)] * 2
        + [jax.ShapeDtypeStruct((size, size), f32)],
        scratch_shapes=[pltpu.VMEM((size, size), bf16)] * 2,
        compiler_params=params(),
        cost_estimate=cost(
            (9 * size**3 + 3 * size * cols * (size + n)) // 2, size * cols * 2
        ),
        name="prepare",
    )(left_param, weight, *rotations)


def grads_kernel(pieces, grad_pieces, has_prev, starts, offsets, *refs):
    tokens = refs[:pieces]
    grads = refs[pieces : pieces + grad_pieces]
    m_h, m_l, v_h, v_l, *rest = refs[pieces + grad_pieces :]
    if has_prev:
        prev, rest = rest[0], rest[1:]
    left, right, peak, gathered, sems = rest
    span = tokens[0].shape[1]
    step = pl.program_id(0)

    @pl.when(step == 0)
    def _():
        copies = [
            pltpu.make_async_copy(
                tokens[k].at[pl.ds(starts[k], gathered.shape[0]), :],
                gathered.at[:, pl.ds(pl.multiple_of(offsets[k], span), span)],
                sems.at[k],
            )
            for k in range(pieces)
        ]
        for copy in copies:
            copy.start()
        for copy in copies:
            copy.wait()

    depth = grads[0].shape[0]
    value = None
    for k, grad in enumerate(grads):
        part = jnp.dot(
            gathered[:, k * depth : (k + 1) * depth], grad[...], preferred_element_type=f32
        )
        value = part if value is None else value + part
    halves = split(value)
    part = mul(halves, (m_h[...], m_l[...]), ((1,), (1,)))

    @pl.when(step == 0)
    def _():
        left[...] = part

    @pl.when(step != 0)
    def _():
        left[...] += part

    @pl.when(step == pl.num_programs(0) - 1)
    def _():
        peak[...] = jnp.full(peak.shape, jnp.max(jnp.abs(left[...])), f32)

    n = right.shape[-1]
    for b in range(right.shape[0]):
        cut = slice(b * n, (b + 1) * n)
        block = mul(
            (v_h[cut, :], v_l[cut, :]), (halves[0][:, cut], halves[1][:, cut])
        )
        right[b] = prev[b] + block if has_prev else block


def gradients(offsets, tokens, starts, grads, prepared, prev, n, tile):
    size = prepared[0].shape[0]
    depth, cols = grads[0].shape
    total = depth * len(grads)
    pieces = len(tokens)
    wide = pl.BlockSpec((size, tile), lambda j, *_: (0, j))
    tall = pl.BlockSpec((tile, size), lambda j, *_: (j, 0))
    right_spec = pl.BlockSpec((tile // n, n, n), lambda j, *_: (j, 0, 0))
    more = [] if prev is None else [prev]
    return pl.pallas_call(
        functools.partial(grads_kernel, pieces, len(grads), prev is not None, tuple(starts)),
        grid_spec=pltpu.PrefetchScalarGridSpec(
            num_scalar_prefetch=1,
            grid=(cols // tile,),
            in_specs=[pl.BlockSpec(memory_space=pl.ANY)] * pieces
            + [pl.BlockSpec((depth, tile), lambda j, *_: (0, j))] * len(grads)
            + [wide, wide, tall, tall]
            + [right_spec] * len(more),
            out_specs=[
                pl.BlockSpec((size, size), lambda j, *_: (0, 0)),
                right_spec,
                pl.BlockSpec((8, 128), lambda j, *_: (0, 0)),
            ],
            scratch_shapes=[
                pltpu.VMEM((size, total), bf16),
                pltpu.SemaphoreType.DMA((pieces,)),
            ],
        ),
        out_shape=[
            jax.ShapeDtypeStruct((size, size), f32),
            jax.ShapeDtypeStruct((cols // n, n, n), f32),
            jax.ShapeDtypeStruct((8, 128), f32),
        ],
        compiler_params=params(),
        cost_estimate=cost(
            size * cols * (total + 3 * (size + n)) // 2, total * cols * 2
        ),
        name="gradients",
    )(offsets, *tokens, *grads, *prepared, *more)


def powers_kernel(many, param, *outs):
    skews = [-skew_of(param[b]) for b in range(many)]
    halves = [split(s) for s in skews]
    second = [mul(h, h) for h in halves]
    third = [mul(h, split(p)) for h, p in zip(halves, second)]
    unit = eye(param.shape[-1])
    for b in range(many):
        tail = unit / 6 + skews[b] / 24 + second[b] / 120 + third[b] / 720
        for k, value in enumerate((skews[b], second[b], third[b], tail)):
            outs[2 * k][b], outs[2 * k + 1][b] = split(value)


def powers(param):
    count, n, _ = param.shape
    many = max(1, math.gcd(count, 1024 // n))
    block = pl.BlockSpec((many, n, n), lambda i: (i, 0, 0))
    return pl.pallas_call(
        functools.partial(powers_kernel, many),
        grid=(count // many,),
        in_specs=[block],
        out_specs=[block] * 8,
        out_shape=[jax.ShapeDtypeStruct((count, n, n), bf16)] * 8,
        compiler_params=params(),
        cost_estimate=cost(count * 6 * n**3, count * n * n * 20),
        name="powers",
    )(param)


def adjoint_kernel(many, grad, *refs):
    *power_refs, out = refs
    sets = [
        [(power_refs[2 * k][b], power_refs[2 * k + 1][b]) for k in range(4)] for b in range(many)
    ]
    grads = [grad[b] for b in range(many)]
    halves = [split(g) for g in grads]
    d_second = [mul(h, s[0]) + mul(s[0], h) for h, s in zip(halves, sets)]
    d_third = [mul(split(d), s[0]) + mul(s[1], h) for d, h, s in zip(d_second, halves, sets)]
    n = grad.shape[-1]
    scale = 0.5 / math.sqrt(n)
    for b in range(many):
        d_tail = grads[b] / 24 + d_second[b] / 120 + d_third[b] / 720
        accum = (
            grads[b]
            + d_second[b] / 2
            + mul(split(d_third[b]), sets[b][3])
            + mul(sets[b][2], split(d_tail))
        )
        skewed = scale * (accum - accum.T)
        mean = jnp.sum(skewed * skewed, keepdims=True) * (1.0 / (n * n))
        skewed = skewed / jnp.sqrt(mean + epsilon)
        out[b, :, : n // 2], out[b, :, n // 2 :] = pack(skewed)


def directions(grad, power_list):
    count, n, _ = grad.shape
    many = max(1, math.gcd(count, 512 // n))
    block = pl.BlockSpec((many, n, n), lambda i: (i, 0, 0))
    return pl.pallas_call(
        functools.partial(adjoint_kernel, many),
        grid=(count // many,),
        in_specs=[block] * 9,
        out_specs=pl.BlockSpec((many, n // 2, n), lambda i: (i, 0, 0)),
        out_shape=jax.ShapeDtypeStruct((count, n // 2, n), f32),
        compiler_params=params(),
        cost_estimate=cost(count * 18 * n**3, count * n * n * 22),
        name="directions",
    )(grad, *power_list)


def turn_kernel(weight, rot_h, rot_l, out_h, out_l):
    halves = split(weight[...])
    n = rot_h.shape[-1]
    for b in range(rot_h.shape[0]):
        cut = slice(b * n, (b + 1) * n)
        out_h[:, cut], out_l[:, cut] = split(
            mul((halves[0][:, cut], halves[1][:, cut]), (rot_h[b], rot_l[b]))
        )


def turn_right(weight, rotations, high, tile):
    rows, cols = weight.shape
    n = rotations[0].shape[-1]
    rot_spec = pl.BlockSpec((tile // n, n, n), lambda j, i: (j, 0, 0))
    spec = pl.BlockSpec((high, tile), lambda j, i: (i, j))
    return pl.pallas_call(
        turn_kernel,
        grid=(cols // tile, rows // high),
        in_specs=[spec, rot_spec, rot_spec],
        out_specs=[spec, spec],
        out_shape=[jax.ShapeDtypeStruct((rows, cols), bf16)] * 2,
        compiler_params=params(2),
        cost_estimate=cost(3 * rows * cols * n, rows * cols * 8),
        name="turn_right",
    )(weight, *rotations)


def left_kernel(many, order, param, skew, packed, new, high, low):
    base = pl.program_id(0) * many
    size = param.shape[-1]
    skews = []
    for b in range(many):
        step = unpack(packed[order[base + b]])
        new[b] = param[b] - step_rate * step
        skews.append(skew[b] - (step_rate / math.sqrt(size)) * step)
    for b, value in enumerate(exponentials(skews)):
        high[b], low[b] = split(value)


def left_rotations(order, param, skews, packed):
    count, size, _ = param.shape
    many = math.gcd(count, 2)
    block = pl.BlockSpec((many, size, size), lambda i, o: (i, 0, 0))
    half = jax.ShapeDtypeStruct((count, size, size), bf16)
    return pl.pallas_call(
        functools.partial(left_kernel, many),
        grid_spec=pltpu.PrefetchScalarGridSpec(
            num_scalar_prefetch=1,
            grid=(count // many,),
            in_specs=[block, block, pl.BlockSpec(packed.shape, lambda i, o: (0, 0, 0))],
            out_specs=[block] * 3,
        ),
        out_shape=[jax.ShapeDtypeStruct((count, size, size), f32), half, half],
        compiler_params=params(),
        cost_estimate=cost(count * 9 * size**3, count * size * size * 14),
        name="left_rotations",
    )(order, param, skews, packed)


def final_kernel(rot_h, rot_l, turned_h, turned_l, out):
    out[...] = mul((rot_h[0], rot_l[0]), (turned_h[...], turned_l[...]))


def finish(rotations, turned, tile):
    count, size, _ = rotations[0].shape
    rows, cols = turned[0].shape
    wide = pl.BlockSpec((size, tile), lambda i, j: (i, j))
    square = pl.BlockSpec((1, size, size), lambda i, j: (i, 0, 0))
    return pl.pallas_call(
        final_kernel,
        grid=(count, cols // tile),
        in_specs=[square, square, wide, wide],
        out_specs=wide,
        out_shape=jax.ShapeDtypeStruct((rows, cols), f32),
        compiler_params=params(2),
        cost_estimate=cost(3 * rows * cols * size, rows * cols * 8),
        name="finish",
    )(*rotations, *turned)


def swap(value, axis):
    count = lax.axis_size(axis)
    return lax.ppermute(value, axis, [(d, d ^ 1) for d in range(count)])


def shift(value, axis, by=1):
    count = lax.axis_size(axis)
    return lax.ppermute(value, axis, [(d, (d + 2 * by) % count) for d in range(count)])


def pick(value, index, axis=0):
    return lax.dynamic_index_in_dim(value, index, axis, keepdims=False)


def gather_pieces(value, axis, kernels=()):
    count = lax.axis_size(axis)
    me = lax.axis_index(axis)
    pieces, sources = [], []
    held = value
    for hop in range(count // 2):
        if hop:
            held = shift(held, axis)
            if kernels:
                held = after(held, kernels[min(len(kernels) - 1, hop + 1)])
        source = (me - 2 * hop + count) % count
        pieces += [held, swap(held, axis)]
        sources += [source, source ^ 1]
    return pieces, sources


def sum_over_groups(parts, axis):
    groups = lax.axis_size(axis) // 2
    mine = lax.axis_index(axis) // 2
    total = pick(parts, mine)
    for by in range(1, groups):
        total = total + shift(pick(parts, (mine + by) % groups), axis, by)
    return total


top = 30000.0


def squared(value, order):
    return (value * jnp.abs(value) * (60000.0 / (0.5 * order**2))).astype(jnp.float16)


def rooted(sent, order):
    value = sent.astype(f32)
    return jnp.sign(value) * jnp.sqrt(jnp.abs(value) * ((0.5 * order**2) / 60000.0))


def after(value, *others):
    return lax.optimization_barrier((value, *others))[0]


def body(tokens, grad_out, base_weight, left_param, right_param):
    col_count = lax.axis_size("col")
    row_count = lax.axis_size("row")
    col = lax.axis_index("col")
    row = lax.axis_index("row")
    left_count, size, _ = left_param.shape
    right_count, n, _ = right_param.shape
    rows, cols = base_weight.shape
    tile = math.gcd(cols, 512)
    groups = col_count // 2
    left_split = left_count % groups == 0
    right_split = right_count % row_count == 0

    turned_tokens = tokens.T
    rotations = right_rotations(right_param)
    kernels = []
    prepared, skews = [], []

    def prepare_next(*held_back):
        i = len(prepared)
        held_back += tuple(kernels[-1:])
        param = after(left_param, *held_back) if held_back else left_param
        *made, skew = prepare(i, param, base_weight, rotations, tile)
        prepared.append(made)
        skews.append(skew)
        kernels.append(skew)

    right_part = None
    sent_parts, others, left_parts, peaks = [], [], [], []

    def gradients_next(*held_back):
        nonlocal right_part
        i = len(left_parts)
        made = lax.optimization_barrier((*prepared[i], *held_back))[:4]
        here = [(p[i * len(p) // left_count], i % (left_count // len(p)) * size) for p in pieces]
        left_part, right_part, peak = gradients(
            offsets,
            [p for p, _ in here],
            [start for _, start in here],
            grads,
            made,
            right_part,
            n,
            tile,
        )
        left_parts.append(left_part)
        peaks.append(peak)
        kernels.append(left_part)
        if left_split:
            shaped = left_part.reshape(2, size // 2, size)
            sent_parts.append(pick(shaped, 1 - col % 2))
            others.append(swap(sent_parts[-1], "col"))

    own_powers = []

    def powers_next(*ties):
        held = lax.optimization_barrier(
            (own_left, own_right, jnp.stack(skews), kernels[-1], *ties)
        )
        left_powers = powers(held[0])
        right_powers = powers(after(held[1], left_powers[0]))
        own_powers[:] = [left_powers, right_powers, held[2]]
        kernels.append(right_powers[0])

    grads, grad_sources = [], []
    me = lax.axis_index("col")
    sources = []
    for hop in range(groups):
        source = (me - 2 * hop + col_count) % col_count
        sources += [source, source ^ 1]
    if left_split:
        left_own = left_count // groups
        own_left = lax.dynamic_slice_in_dim(left_param, (col // 2) * left_own, left_own, 0)
    else:
        own_left = left_param
    if right_split:
        right_own = right_count // row_count
        own_right = lax.dynamic_slice_in_dim(right_param, row * right_own, right_own, 0)
    else:
        own_right = right_param

    pieces = []
    swapped = []
    offsets = None

    def gather_grads():
        nonlocal offsets
        grads[:], grad_sources[:] = gather_pieces(grad_out, "row", kernels)
        span = grad_out.shape[0]
        place = jnp.zeros((row_count,), jnp.int32)
        for k, source in enumerate(grad_sources):
            place = jnp.where(jnp.arange(row_count) == source, k, place)
        first = jnp.stack(sources).astype(jnp.int32) * tokens.shape[0]
        offsets = place[first // span] * span + first % span

    held = turned_tokens
    half = rows // 2
    for hop in range(groups):
        if hop:
            held = after(shift(held, "col"), kernels[-1])
        ties = [held] + swapped[-1:] if hop else []
        pieces.append((held,))
        if 0 < hop == groups - 1 and left_count % 2 == 0:
            behind = after(swapped[-1][half:], kernels[-1])
            pieces.append((swap(held[:half], "col"), shift(behind, "col")))
            powers_next(*ties)
        else:
            swapped.append(swap(held, "col"))
            pieces.append(swapped[-1:])
        while len(prepared) < left_count and hop >= (len(prepared) + 1) // 2:
            prepare_next(*ties)
    while len(prepared) < left_count:
        prepare_next()
    gather_grads()
    if not own_powers:
        powers_next()
    left_powers, right_powers, skews = own_powers
    ties = [left_powers[0]]
    while len(left_parts) < left_count:
        gradients_next(*ties)
        ties = sent_parts[-1:] + others[-2:-1]

    left_halves = []
    if left_split:
        for left_part, other in zip(left_parts, others):
            shaped = left_part.reshape(2, size // 2, size)
            left_halves.append(pick(shaped, col % 2) + other)

    if right_split:
        outer = row_count // 2
        shaped = right_part.reshape(outer, 2, right_own, n, n)
        mine = pick(shaped, row % 2, 1) + swap(pick(shaped, 1 - row % 2, 1), "row")
        right_grad = sum_over_groups(mine, "row")
    else:
        right_grad = lax.psum(right_part, "row")

    right_packed = directions(right_grad, right_powers)
    if right_split:
        held, sources = gather_pieces(right_packed, "row")
        packed_all = jnp.concatenate(held, 0)
        place = jnp.zeros((row_count,), jnp.int32)
        for k, source in enumerate(sources):
            place = place + jnp.where(jnp.arange(row_count) == source, k, 0)
        right_order = (
            place[:, None] * right_own + jnp.arange(right_own)[None, :]
        ).reshape(-1).astype(jnp.int32)
    else:
        packed_all = right_packed
        right_order = jnp.arange(right_count, dtype=jnp.int32)

    if left_split:
        halves = jnp.stack(left_halves).reshape(groups, left_own, size // 2, size)
        group = col // 2
        most = functools.reduce(jnp.maximum, peaks)
        most = jnp.maximum(most + swap(most, "col"), 1e-30)
        mine = pick(halves, group)
        for by in range(1, groups):
            sent = pick(halves, (group + by) % groups) * (top / most[0, 0])
            theirs = shift(most, "col", by)[0, 0] / top
            mine = mine + shift(sent.astype(jnp.float16), "col", by).astype(f32) * theirs
        other = swap(mine, "col")
        first = jnp.where(col % 2 == 0, mine, other)
        last = jnp.where(col % 2 == 0, other, mine)
        left_grad = jnp.concatenate([first, last], 1)
    else:
        left_grad = lax.psum(jnp.stack(left_parts), "col")

    left_packed = directions(after(left_grad, right_packed), left_powers)
    if left_split:
        sent = squared(left_packed, size)
        held = [sent] + [shift(sent, "col", by) for by in range(1, groups)]
        block = jnp.arange(left_count)
        back = (group - block // left_own + groups) % groups
        left_order = (back * left_own + block % left_own).astype(jnp.int32)
        packed_all = after(packed_all, left_packed)
    else:
        left_all = left_packed
        left_order = jnp.arange(left_count, dtype=jnp.int32)
    new_right, *new_rotations = right_rotations(right_param, packed_all, right_order)
    turned = turn_right(base_weight, new_rotations, math.gcd(rows, 512), math.gcd(cols, 2048))
    if left_split:
        held = lax.optimization_barrier((*held, turned[0]))[:-1]
        left_all = rooted(jnp.concatenate(held, 0), size)
    new_left, *left_rots = left_rotations(left_order, left_param, skews, left_all)
    rotated_weight = finish(left_rots, turned, math.gcd(cols, 2048))
    return (rotated_weight, new_left, new_right)


def solution(mesh):
    return jax.shard_map(
        body,
        mesh=mesh,
        in_specs=(
            P("col", "row"),
            P("row", "col"),
            P("row", "col"),
            P("row", None, None),
            P("col", None, None),
        ),
        out_specs=(P("row", "col"), P("row", None, None), P("col", None, None)),
        check_vma=False,
    )
```
